32 devices in a mesh: row: 4 (over z), col: 8 (over y, x, core).
Axes of the slice: x: 2, y: 2, z: 4, core: 2. Of those that a mesh axis runs over, the one named last changes fastest.
Arguments:
- a_matrix: float32 [1024, 3072], P('row', 'col'), may hold values from -6 to 6
- b_matrix: float32 [1024, 3072], P('row', 'col'), as said below
Outputs:
- a_result: float32 [1024, 3072], P('row', 'col')
- b_result: float32 [1024, 3072], P('row', 'col')
The draws below stay inside these ranges and needn't reach their ends.
Inputs may be any that keep to these rules, and one draw needn't show every extreme that they name: b_matrix is zero in its first 256 columns and, at the window's columns t, zero in rows below t; its entry in row t at window column t lies between 4 and 8.
All inputs are finite; a program needn't handle non-finite values.
Results may differ from the reference program's by a relative error of at most 0.00023.
Values sent between devices are 32-bit elements; how exact they have to be, the bound alone decides.
A program may use at most 64 MiB of HBM per device.

```python
import math
import jax
import jax.numpy as jnp
from jax import lax

NB = 256
CB = 384
M = 1024
NCOLS = 3072
N_COL = 8


def draw_b_matrix(key, part):
    noise_key = jax.random.fold_in(key, 11)
    diag_key = jax.random.fold_in(key, 23)
    scale = 1.5 / math.sqrt(M)
    noise = jnp.clip(jax.random.normal(noise_key, (M, NCOLS), jnp.float32), -4.0, 4.0)
    noise = noise * scale
    diagonal = 4.0 * jnp.exp(jnp.log(2.0) * jax.random.uniform(diag_key, (M, 1), jnp.float32))
    width_dev = M // N_COL
    rows = jnp.arange(M)[:, None]
    columns = jnp.arange(NCOLS)[None, :]
    local = columns % CB
    inside = local >= CB - width_dev
    position = columns // CB * width_dev + local - (CB - width_dev)
    values = jnp.where(inside & (position == rows), diagonal, noise)
    values = jnp.where(inside & (position < rows), 0.0, values)
    values = jnp.where(columns < NB, 0.0, values)
    return values.astype(jnp.float32)


def shard_levels(key, dims, pieces, smallest, high):
    level, own = 1.0, jax.random.fold_in(key, 6)
    for dim, shards_of in pieces:
        heights = jnp.exp(jax.random.uniform(jax.random.fold_in(own, dim), (shards_of,), jnp.float32, smallest / len(pieces), high / len(pieces)))
        level = level * jnp.repeat(heights, dims[dim] // shards_of).reshape([-1 if axis == dim else 1 for axis in range(len(dims))])
    return level


def gaussian(key, shape, deviation, limit, shards=(), kind=jnp.bfloat16):
    level = shard_levels(key, shape, shards, -0.22, 0.18) if shards else 1.0
    drawn = jax.random.normal(key, shape, jnp.float32) * deviation * level
    return jnp.minimum(jnp.maximum(drawn, -limit), limit).astype(kind)


def setup_inputs(seed: int = 0) -> dict:
    key_list = jax.random.split(jax.random.key(seed), 3)
    a_matrix = gaussian(key_list[0], (M, NCOLS), 1.0, 6.0, ((0, 4), (1, 8)), jnp.float32)
    b_matrix = draw_b_matrix(jax.random.fold_in(key_list[2], 71), 0)
    return dict(a_matrix=a_matrix, b_matrix=b_matrix)


def product(left_side, right_side):
    return jnp.dot(left_side.astype(jnp.float32), right_side.astype(jnp.float32), precision=lax.Precision.HIGHEST, preferred_element_type=jnp.float32)

def tri_solve(factor, values, on_left, transpose):
    return lax.linalg.triangular_solve(factor, values, left_side=on_left, lower=True, transpose_a=transpose)

def inverse_of(square):
    normal = product(square.T, square)
    factor = jnp.linalg.cholesky(normal)
    first = tri_solve(factor, square.T, True, False)
    return tri_solve(factor, first, True, True)

def lower_from_reversed(gram):
    factor = jnp.linalg.cholesky(gram[::-1, ::-1])
    return factor.T[::-1, ::-1]

def reference(a_matrix, b_matrix):
    identity = jnp.eye(NB, dtype=jnp.float32)
    panel = a_matrix[:, :NB]
    factor = jnp.linalg.cholesky(product(panel.T, panel))
    q_panel = tri_solve(factor, panel, False, True)
    w_left = q_panel.at[:NB].add(identity)
    k_left = inverse_of(identity + q_panel[:NB])
    a_left = a_matrix - product(w_left, product(k_left, product(w_left.T, a_matrix)))
    b_left = b_matrix - product(w_left, product(k_left, product(w_left.T, b_matrix)))
    width_dev = M // N_COL
    positions = jnp.arange(M, dtype=jnp.int32)
    window_cols = (positions // width_dev * CB + (CB - width_dev) + positions % width_dev).astype(jnp.int32)
    strip = jnp.take(b_left[M - NB:], window_cols, axis=1)
    right_factor = lower_from_reversed(product(strip, strip.T))
    q_strip = tri_solve(right_factor, strip.T, False, False)
    w_right = q_strip.at[M - NB:].add(identity)
    k_right = inverse_of(identity + q_strip[M - NB:].T)
    results = []
    for current in (a_left, b_left):
        window = jnp.take(current, window_cols, axis=1)
        window = window - product(product(product(window, w_right), k_right), w_right.T)
        results.append(current.at[:, window_cols].set(window))
    return (results[0], results[1])
```

```python
import functools

import jax
import jax.numpy as jnp
from jax import lax
from jax.experimental import pallas as pl
from jax.experimental.pallas import tpu as pltpu
from jax.sharding import PartitionSpec as P

NB = 256
HB = NB // 2
MESH = pl.DeviceIdType.MESH


def dot(x, y, cx=1, cy=0):
    return lax.dot_general(
        x,
        y,
        (((cx,), (cy,)), ((), ())),
        precision=lax.Precision.HIGHEST,
        preferred_element_type=jnp.float32,
    )


def iotas():
    rows = lax.broadcasted_iota(jnp.int32, (HB, HB), 0)
    cols = lax.broadcasted_iota(jnp.int32, (HB, HB), 1)
    return rows, cols


def invert_half(a):
    rows, cols = iotas()
    for j in range(HB):
        inv = 1.0 / a[j : j + 1, j : j + 1]
        row = jnp.where(cols[:1] == j, 1.0, a[j : j + 1, :]) * inv
        col = jnp.where(rows[:, :1] == j, -1.0, a[:, j : j + 1])
        kept = jnp.where((rows == j) | (cols == j), 0.0, a)
        a = kept - col * row
    return a


def invert(m):
    a, b = m[:HB, :HB], m[:HB, HB:]
    c, d = m[HB:, :HB], m[HB:, HB:]
    ai = invert_half(a)
    cai = dot(c, ai)
    aib = dot(ai, b)
    si = invert_half(d - dot(cai, b))
    low = dot(si, cai)
    right = dot(aib, si)
    top = jnp.concatenate([ai + dot(aib, low), -right], axis=1)
    return jnp.concatenate([top, jnp.concatenate([-low, si], axis=1)], axis=0)


def eliminate_half(a, reverse):
    rows, cols = iotas()
    order = range(HB - 1, -1, -1) if reverse else range(HB)
    for j in order:
        inv = 1.0 / a[j : j + 1, j : j + 1]
        row = jnp.where(cols[:1] == j, 1.0, a[j : j + 1, :]) * inv
        todo = rows < j if reverse else rows > j
        col = jnp.where(todo[:, :1], a[:, j : j + 1], 0.0)
        a = jnp.where(todo & (cols == j), 0.0, a) - col * row
    diag = jnp.sum(jnp.where(rows == cols, a, 0.0), axis=1, keepdims=True)
    scale = 1.0 / jnp.sqrt(diag)
    keep = rows >= cols if reverse else rows <= cols
    factor = jnp.where(keep, a, 0.0) * scale
    inverse = jnp.where(keep, jnp.where(rows == cols, 1.0, 0.0), a) * scale
    return factor, inverse


def factor_kernel(reverse, g_ref, o_ref):
    g = g_ref[...]
    a, b = g[:HB, :HB], g[:HB, HB:]
    c, d = g[HB:, :HB], g[HB:, HB:]
    zero = jnp.zeros((HB, HB), jnp.float32)
    if reverse:
        f2, inv2 = eliminate_half(d, True)
        low = dot(inv2, c)
        f1, _ = eliminate_half(a - dot(low, low, 0, 0), True)
        o_ref[...] = jnp.concatenate(
            [jnp.concatenate([f1, zero], axis=1), jnp.concatenate([low, f2], axis=1)], axis=0
        )
    else:
        f1, inv1 = eliminate_half(a, False)
        up = dot(inv1, b)
        f2, _ = eliminate_half(d - dot(up, up, 0, 0), False)
        o_ref[...] = jnp.concatenate(
            [jnp.concatenate([f1, up], axis=1), jnp.concatenate([zero, f2], axis=1)], axis=0
        )


VM = pl.BlockSpec(memory_space=pltpu.VMEM)
LIMIT = 48 * 1024 * 1024


def factor(gram, reverse):
    return pl.pallas_call(
        functools.partial(factor_kernel, reverse),
        out_shape=jax.ShapeDtypeStruct((NB, NB), jnp.float32),
        in_specs=[VM],
        out_specs=VM,
        compiler_params=pltpu.CompilerParams(vmem_limit_bytes=LIMIT),
        name="factor_rev" if reverse else "factor_fwd",
    )(gram)


def greet(axis, n):
    me = lax.axis_index(axis)
    barrier = pltpu.get_barrier_semaphore()
    for d in range(1, n):
        pl.semaphore_signal(
            barrier, inc=1, device_id={axis: lax.rem(me + d, n)}, device_id_type=MESH
        )
    pl.semaphore_wait(barrier, n - 1)
    return me


def send_all(axis, n, me, source, target, send_sem, recv_sem):
    copies = []
    for d in range(1, n):
        peer = lax.rem(me + d, n)
        copy = pltpu.make_async_remote_copy(
            src_ref=source(peer),
            dst_ref=target.at[me],
            send_sem=send_sem.at[d - 1],
            recv_sem=recv_sem.at[d - 1],
            device_id={axis: peer},
            device_id_type=MESH,
        )
        copy.start()
        copies.append(copy)
    return copies


def exchange_kernel(axis, n, gather, x_ref, o_ref, send_sem, recv_sem):
    me = greet(axis, n)
    source = (lambda peer: x_ref) if gather else (lambda peer: x_ref.at[peer])
    copies = send_all(axis, n, me, source, o_ref, send_sem, recv_sem)
    o_ref[me] = x_ref[...] if gather else x_ref[me]
    for copy in copies:
        copy.wait()


def exchange(x, axis, gather, collective_id):
    n = lax.axis_size(axis)
    shape = (n,) + x.shape if gather else x.shape
    return pl.pallas_call(
        functools.partial(exchange_kernel, axis, n, gather),
        out_shape=jax.ShapeDtypeStruct(shape, jnp.float32),
        in_specs=[VM],
        out_specs=VM,
        scratch_shapes=[pltpu.SemaphoreType.DMA((n - 1,)), pltpu.SemaphoreType.DMA((n - 1,))],
        compiler_params=pltpu.CompilerParams(
            collective_id=collective_id, has_side_effects=True, vmem_limit_bytes=LIMIT
        ),
        name=("gather_" if gather else "scatter_") + axis + str(collective_id),
    )(x)


def reduce_solve_kernel(axis, n, z_ref, m_ref, o_ref, got, s1, r1, s2, r2):
    me = greet(axis, n)
    copies = send_all(axis, n, me, lambda peer: z_ref.at[peer], got, s1, r1)
    inverse = invert(m_ref[...])
    got[me] = z_ref[me]
    for copy in copies:
        copy.wait()
    total = got[0]
    for i in range(1, n):
        total = total + got[i]
    o_ref[me] = dot(total, inverse)
    for copy in send_all(axis, n, me, lambda peer: o_ref.at[me], o_ref, s2, r2):
        copy.wait()


def reduce_solve(z, m, axis, collective_id):
    n = lax.axis_size(axis)
    parts = z.reshape(n, z.shape[0] // n, NB)
    out = pl.pallas_call(
        functools.partial(reduce_solve_kernel, axis, n),
        out_shape=jax.ShapeDtypeStruct(parts.shape, jnp.float32),
        in_specs=[VM, VM],
        out_specs=VM,
        scratch_shapes=[pltpu.VMEM(parts.shape, jnp.float32)]
        + [pltpu.SemaphoreType.DMA((n - 1,))] * 4,
        compiler_params=pltpu.CompilerParams(
            collective_id=collective_id, has_side_effects=True, vmem_limit_bytes=LIMIT
        ),
        name="solve_" + axis,
    )(parts, m)
    return out.reshape(z.shape)


def local(a_matrix, b_matrix):
    rows, block_cols = a_matrix.shape
    n_row, n_col = lax.axis_size("row"), lax.axis_size("col")
    window = NB * n_row // n_col
    start = block_cols - window
    row_place, col_place = lax.axis_index("row"), lax.axis_index("col")
    strip_b = jnp.where(row_place == n_row - 1, b_matrix[:, start:], 0.0)
    strip_b = lax.psum(strip_b, "row")

    chunk = rows // n_col
    mine = exchange(a_matrix[:, :NB].reshape(n_col, chunk, NB), "col", False, 1)[0]
    mine = exchange(mine, "row", True, 2)
    panel = exchange(mine, "col", True, 3)
    panel = jnp.swapaxes(panel, 0, 1).reshape(n_row * rows, NB)
    own_panel = lax.dynamic_slice_in_dim(panel, row_place * rows, rows, 0)
    gram = dot(panel, panel, 0, 0)
    upper = factor(gram, False)
    top = panel[:NB]
    v_rows = own_panel + jnp.where(row_place == 0, upper, 0.0)
    z_left = jnp.concatenate([dot(a_matrix, v_rows, 0, 0), dot(b_matrix, v_rows, 0, 0)], axis=0)
    left = reduce_solve(z_left, gram + dot(top, upper, 0, 0), "row", 4)
    left_a, left_b = left[:block_cols], left[block_cols:]
    last_rows = panel[(n_row - 1) * rows :]
    strip = strip_b - dot(last_rows, left_b[start:], 1, 1)
    strips = exchange(strip, "col", True, 5)
    a_left = a_matrix - dot(v_rows, left_a, 1, 1)
    b_left = b_matrix - dot(v_rows, left_b, 1, 1)

    full = jnp.swapaxes(strips, 0, 1).reshape(NB, n_col * window)
    gram_right = dot(full, full, 1, 1)
    right = factor(gram_right, True)
    m_right = gram_right + dot(full[:, n_col * window - NB :], right)
    n_last = NB // window
    place = col_place - (n_col - n_last)
    added = lax.dynamic_slice_in_dim(right, jnp.maximum(place, 0) * window, window, 0)
    v_cols = strip + jnp.where(place >= 0, added, 0.0).T
    z_right = jnp.concatenate(
        [dot(a_left[:, start:], v_cols, 1, 1), dot(b_left[:, start:], v_cols, 1, 1)], axis=0
    )
    coeff = reduce_solve(z_right, m_right, "col", 6)
    fix = dot(coeff, v_cols)
    a_result = jnp.concatenate([a_left[:, :start], a_left[:, start:] - fix[:rows]], axis=1)
    b_result = jnp.concatenate([b_left[:, :start], b_left[:, start:] - fix[rows:]], axis=1)
    return (a_result, b_result)


def solution(mesh):
    placed = (P("row", "col"), P("row", "col"))
    return jax.shard_map(
        local,
        mesh=mesh,
        in_specs=placed,
        out_specs=(P("row", "col"), P("row", "col")),
        check_vma=False,
    )
```

```python
import functools

import jax
import jax.numpy as jnp
from jax import lax
from jax.experimental import pallas as pl
from jax.experimental.pallas import tpu as pltpu
from jax.sharding import PartitionSpec as P

NB = 256
HB = NB // 2
MESH = pl.DeviceIdType.MESH


def dot(x, y, cx=1, cy=0):
    return lax.dot_general(
        x,
        y,
        (((cx,), (cy,)), ((), ())),
        precision=lax.Precision.HIGHEST,
        preferred_element_type=jnp.float32,
    )


TILE = 8
COUNT = HB // TILE


def spread(x):
    return jnp.broadcast_to(x, (TILE, HB))


def step_tile(tiles, t, order):
    lane = lax.broadcasted_iota(jnp.int32, (TILE, HB), 1) - t * TILE
    inside = (lane >= 0) & (lane < TILE)
    at = [lane == k for k in range(TILE)]
    rows = [spread(tiles[t][k : k + 1, :]) for k in range(TILE)]
    s = [[spread(rows[r][:, t * TILE + k : t * TILE + k + 1]) for k in range(TILE)] for r in range(TILE)]
    rows = [
        jnp.where(inside, jnp.where(at[k], 1.0, 0.0), rows[k]) for k in range(TILE)
    ]
    forward = [None] * TILE
    for i, m in enumerate(order):
        later = order[i + 1 :]
        kept = jnp.where(at[m], s[m][m], rows[m])
        for k in later:
            kept = jnp.where(at[k], s[m][k], kept)
        forward[m] = kept
        inv = 1.0 / s[m][m]
        for k in later:
            s[m][k] = s[m][k] * inv
        for r in later:
            for k in later:
                s[r][k] = s[r][k] - s[r][m] * s[m][k]
        rows[m] = rows[m] * inv
        for r in later:
            rows[r] = rows[r] - s[r][m] * rows[m]
    for i in range(TILE - 1, 0, -1):
        m = order[i]
        for r in order[:i]:
            rows[r] = rows[r] - s[r][m] * rows[m]
    return rows, forward, inside


def apply_tile(tile, t, rows, inside):
    out = jnp.where(inside, 0.0, tile)
    for k in range(TILE):
        out = out - spread(tile[:, t * TILE + k : t * TILE + k + 1]) * rows[k]
    return out


def stack(rows):
    sub = lax.broadcasted_iota(jnp.int32, (TILE, HB), 0)
    out = rows[0]
    for k in range(1, TILE):
        out = jnp.where(sub == k, rows[k], out)
    return out


def invert_half(a):
    tiles = [a[i * TILE : (i + 1) * TILE, :] for i in range(COUNT)]
    order = list(range(TILE))
    for t in range(COUNT):
        rows, _, inside = step_tile(tiles, t, order)
        tiles = [
            stack(rows) if i == t else apply_tile(tiles[i], t, rows, inside)
            for i in range(COUNT)
        ]
    return jnp.concatenate(tiles, axis=0)


def invert(m):
    a, b = m[:HB, :HB], m[:HB, HB:]
    c, d = m[HB:, :HB], m[HB:, HB:]
    ai = invert_half(a)
    cai = dot(c, ai)
    aib = dot(ai, b)
    si = invert_half(d - dot(cai, b))
    low = dot(si, cai)
    right = dot(aib, si)
    top = jnp.concatenate([ai + dot(aib, low), -right], axis=1)
    return jnp.concatenate([top, jnp.concatenate([-low, si], axis=1)], axis=0)


def eliminate_half(a, reverse):
    tiles = [a[i * TILE : (i + 1) * TILE, :] for i in range(COUNT)]
    order, places = list(range(TILE)), list(range(COUNT))
    if reverse:
        order, places = order[::-1], places[::-1]
    for n, t in enumerate(places):
        rows, forward, inside = step_tile(tiles, t, order)
        tiles[t] = stack(forward)
        for i in places[n + 1 :]:
            tiles[i] = apply_tile(tiles[i], t, rows, inside)
    a = jnp.concatenate(tiles, axis=0)
    rows = lax.broadcasted_iota(jnp.int32, (HB, HB), 0)
    cols = lax.broadcasted_iota(jnp.int32, (HB, HB), 1)
    diag = jnp.sum(jnp.where(rows == cols, a, 0.0), axis=1, keepdims=True)
    scale = 1.0 / jnp.sqrt(diag)
    keep = rows >= cols if reverse else rows <= cols
    factor = jnp.where(keep, a, 0.0) * scale
    inverse = jnp.where(keep, jnp.where(rows == cols, 1.0, 0.0), a) * scale
    return factor, inverse


def factor_kernel(reverse, g_ref, o_ref):
    g = g_ref[...]
    a, b = g[:HB, :HB], g[:HB, HB:]
    c, d = g[HB:, :HB], g[HB:, HB:]
    zero = jnp.zeros((HB, HB), jnp.float32)
    if reverse:
        f2, inv2 = eliminate_half(d, True)
        low = dot(inv2, c)
        f1, _ = eliminate_half(a - dot(low, low, 0, 0), True)
        o_ref[...] = jnp.concatenate(
            [jnp.concatenate([f1, zero], axis=1), jnp.concatenate([low, f2], axis=1)], axis=0
        )
    else:
        f1, inv1 = eliminate_half(a, False)
        up = dot(inv1, b)
        f2, _ = eliminate_half(d - dot(up, up, 0, 0), False)
        o_ref[...] = jnp.concatenate(
            [jnp.concatenate([f1, up], axis=1), jnp.concatenate([zero, f2], axis=1)], axis=0
        )


VM = pl.BlockSpec(memory_space=pltpu.VMEM)
LIMIT = 48 * 1024 * 1024


def factor(gram, reverse):
    return pl.pallas_call(
        functools.partial(factor_kernel, reverse),
        out_shape=jax.ShapeDtypeStruct((NB, NB), jnp.float32),
        in_specs=[VM],
        out_specs=VM,
        compiler_params=pltpu.CompilerParams(vmem_limit_bytes=LIMIT),
        name="factor_rev" if reverse else "factor_fwd",
    )(gram)


def greet(axis, n):
    me = lax.axis_index(axis)
    barrier = pltpu.get_barrier_semaphore()
    for d in range(1, n):
        pl.semaphore_signal(
            barrier, inc=1, device_id={axis: lax.rem(me + d, n)}, device_id_type=MESH
        )
    pl.semaphore_wait(barrier, n - 1)
    return me


def send_all(axis, n, me, source, target, send_sem, recv_sem):
    copies = []
    for d in range(1, n):
        peer = lax.rem(me + d, n)
        copy = pltpu.make_async_remote_copy(
            src_ref=source(peer),
            dst_ref=target.at[me],
            send_sem=send_sem.at[d - 1],
            recv_sem=recv_sem.at[d - 1],
            device_id={axis: peer},
            device_id_type=MESH,
        )
        copy.start()
        copies.append(copy)
    return copies


def gather_pairs(axis, n, me, source, target, send_sem, recv_sem):
    partner = me + 1 - 2 * lax.rem(me, 2)

    def copy_to(src, slot, index, peer):
        copy = pltpu.make_async_remote_copy(
            src_ref=src,
            dst_ref=target.at[slot],
            send_sem=send_sem.at[index],
            recv_sem=recv_sem.at[index],
            device_id={axis: peer},
            device_id_type=MESH,
        )
        copy.start()
        return copy

    half = n // 2
    first = [copy_to(source, me, d - 1, lax.rem(me + 2 * d, n)) for d in range(1, half)]
    rest = [copy_to(source, me, half - 1, partner)]
    for d in range(1, half):
        first[d - 1].wait_recv()
        slot = lax.rem(me + n - 2 * d, n)
        rest.append(copy_to(target.at[slot], slot, half - 1 + d, partner))
    for copy in first:
        copy.wait_send()
    for copy in rest:
        copy.wait()


def exchange_kernel(axis, n, gather, x_ref, o_ref, send_sem, recv_sem):
    me = greet(axis, n)
    if gather and axis == "col":
        o_ref[me] = x_ref[...]
        gather_pairs(axis, n, me, x_ref, o_ref, send_sem, recv_sem)
        return
    source = (lambda peer: x_ref) if gather else (lambda peer: x_ref.at[peer])
    copies = send_all(axis, n, me, source, o_ref, send_sem, recv_sem)
    o_ref[me] = x_ref[...] if gather else x_ref[me]
    for copy in copies:
        copy.wait()


def exchange(x, axis, gather, collective_id):
    n = lax.axis_size(axis)
    shape = (n,) + x.shape if gather else x.shape
    return pl.pallas_call(
        functools.partial(exchange_kernel, axis, n, gather),
        out_shape=jax.ShapeDtypeStruct(shape, jnp.float32),
        in_specs=[VM],
        out_specs=VM,
        scratch_shapes=[pltpu.SemaphoreType.DMA((n - 1,)), pltpu.SemaphoreType.DMA((n - 1,))],
        compiler_params=pltpu.CompilerParams(
            collective_id=collective_id, has_side_effects=True, vmem_limit_bytes=LIMIT
        ),
        name=("gather_" if gather else "scatter_") + axis + str(collective_id),
    )(x)


def reduce_solve_kernel(axis, n, z_ref, m_ref, o_ref, got, s1, r1, s2, r2):
    me = greet(axis, n)
    copies = send_all(axis, n, me, lambda peer: z_ref.at[peer], got, s1, r1)
    inverse = invert(m_ref[...])
    got[me] = z_ref[me]
    for copy in copies:
        copy.wait()
    total = got[0]
    for i in range(1, n):
        total = total + got[i]
    o_ref[me] = dot(total, inverse)
    if axis == "col":
        gather_pairs(axis, n, me, o_ref.at[me], o_ref, s2, r2)
        return
    for copy in send_all(axis, n, me, lambda peer: o_ref.at[me], o_ref, s2, r2):
        copy.wait()


def reduce_solve(z, m, axis, collective_id):
    n = lax.axis_size(axis)
    parts = z.reshape(n, z.shape[0] // n, NB)
    out = pl.pallas_call(
        functools.partial(reduce_solve_kernel, axis, n),
        out_shape=jax.ShapeDtypeStruct(parts.shape, jnp.float32),
        in_specs=[VM, VM],
        out_specs=VM,
        scratch_shapes=[pltpu.VMEM(parts.shape, jnp.float32)]
        + [pltpu.SemaphoreType.DMA((n - 1,))] * 4,
        compiler_params=pltpu.CompilerParams(
            collective_id=collective_id, has_side_effects=True, vmem_limit_bytes=LIMIT
        ),
        name="solve_" + axis,
    )(parts, m)
    return out.reshape(z.shape)


def local(a_matrix, b_matrix):
    rows, block_cols = a_matrix.shape
    n_row, n_col = lax.axis_size("row"), lax.axis_size("col")
    window = NB * n_row // n_col
    start = block_cols - window
    row_place, col_place = lax.axis_index("row"), lax.axis_index("col")
    strip_b = jnp.where(row_place == n_row - 1, b_matrix[:, start:], 0.0)
    strip_b = lax.psum(strip_b, "row")

    chunk = rows // n_col
    mine = exchange(a_matrix[:, :NB].reshape(n_col, chunk, NB), "col", False, 1)[0]
    mine = exchange(mine, "row", True, 2)
    panel = exchange(mine, "col", True, 3)
    panel = jnp.swapaxes(panel, 0, 1).reshape(n_row * rows, NB)
    own_panel = lax.dynamic_slice_in_dim(panel, row_place * rows, rows, 0)
    gram = dot(panel, panel, 0, 0)
    upper = factor(gram, False)
    top = panel[:NB]
    v_rows = own_panel + jnp.where(row_place == 0, upper, 0.0)
    z_left = jnp.concatenate([dot(a_matrix, v_rows, 0, 0), dot(b_matrix, v_rows, 0, 0)], axis=0)
    left = reduce_solve(z_left, gram + dot(top, upper, 0, 0), "row", 4)
    left_a, left_b = left[:block_cols], left[block_cols:]
    last_rows = panel[(n_row - 1) * rows :]
    strip = strip_b - dot(last_rows, left_b[start:], 1, 1)
    strips = exchange(strip, "col", True, 5)
    a_left = a_matrix - dot(v_rows, left_a, 1, 1)
    b_left = b_matrix - dot(v_rows, left_b, 1, 1)

    full = jnp.swapaxes(strips, 0, 1).reshape(NB, n_col * window)
    gram_right = dot(full, full, 1, 1)
    right = factor(gram_right, True)
    m_right = gram_right + dot(full[:, n_col * window - NB :], right)
    n_last = NB // window
    place = col_place - (n_col - n_last)
    added = lax.dynamic_slice_in_dim(right, jnp.maximum(place, 0) * window, window, 0)
    v_cols = strip + jnp.where(place >= 0, added, 0.0).T
    z_right = jnp.concatenate(
        [dot(a_left[:, start:], v_cols, 1, 1), dot(b_left[:, start:], v_cols, 1, 1)], axis=0
    )
    coeff = reduce_solve(z_right, m_right, "col", 6)
    fix = dot(coeff, v_cols)
    a_result = jnp.concatenate([a_left[:, :start], a_left[:, start:] - fix[:rows]], axis=1)
    b_result = jnp.concatenate([b_left[:, :start], b_left[:, start:] - fix[rows:]], axis=1)
    return (a_result, b_result)


def solution(mesh):
    placed = (P("row", "col"), P("row", "col"))
    return jax.shard_map(
        local,
        mesh=mesh,
        in_specs=placed,
        out_specs=(P("row", "col"), P("row", "col")),
        check_vma=False,
    )
```

```python
import functools

import jax
import jax.numpy as jnp
from jax import lax
from jax.experimental import pallas as pl
from jax.experimental.pallas import tpu as pltpu
from jax.sharding import PartitionSpec as P

NB = 256
HB = NB // 2
MESH = pl.DeviceIdType.MESH


def dot(x, y, cx=1, cy=0):
    return lax.dot_general(
        x,
        y,
        (((cx,), (cy,)), ((), ())),
        precision=lax.Precision.HIGHEST,
        preferred_element_type=jnp.float32,
    )


TILE = 8
COUNT = HB // TILE


def spread(x):
    return jnp.broadcast_to(x, (TILE, HB))


def step_tile(tiles, t, order):
    lane = lax.broadcasted_iota(jnp.int32, (TILE, HB), 1) - t * TILE
    inside = (lane >= 0) & (lane < TILE)
    at = [lane == k for k in range(TILE)]
    rows = [spread(tiles[t][k : k + 1, :]) for k in range(TILE)]
    s = [[spread(rows[r][:, t * TILE + k : t * TILE + k + 1]) for k in range(TILE)] for r in range(TILE)]
    rows = [
        jnp.where(inside, jnp.where(at[k], 1.0, 0.0), rows[k]) for k in range(TILE)
    ]
    forward = [None] * TILE
    for i, m in enumerate(order):
        later = order[i + 1 :]
        kept = jnp.where(at[m], s[m][m], rows[m])
        for k in later:
            kept = jnp.where(at[k], s[m][k], kept)
        forward[m] = kept
        inv = 1.0 / s[m][m]
        for k in later:
            s[m][k] = s[m][k] * inv
        for r in later:
            for k in later:
                s[r][k] = s[r][k] - s[r][m] * s[m][k]
        rows[m] = rows[m] * inv
        for r in later:
            rows[r] = rows[r] - s[r][m] * rows[m]
    for i in range(TILE - 1, 0, -1):
        m = order[i]
        for r in order[:i]:
            rows[r] = rows[r] - s[r][m] * rows[m]
    return rows, forward, inside


def apply_tile(tile, t, rows, inside):
    out = jnp.where(inside, 0.0, tile)
    for k in range(TILE):
        out = out - spread(tile[:, t * TILE + k : t * TILE + k + 1]) * rows[k]
    return out


def stack(rows):
    sub = lax.broadcasted_iota(jnp.int32, (TILE, HB), 0)
    out = rows[0]
    for k in range(1, TILE):
        out = jnp.where(sub == k, rows[k], out)
    return out


def invert_half(a):
    tiles = [a[i * TILE : (i + 1) * TILE, :] for i in range(COUNT)]
    order = list(range(TILE))
    for t in range(COUNT):
        rows, _, inside = step_tile(tiles, t, order)
        tiles = [
            stack(rows) if i == t else apply_tile(tiles[i], t, rows, inside)
            for i in range(COUNT)
        ]
    return jnp.concatenate(tiles, axis=0)


def invert(m):
    a, b = m[:HB, :HB], m[:HB, HB:]
    c, d = m[HB:, :HB], m[HB:, HB:]
    ai = invert_half(a)
    cai = dot(c, ai)
    aib = dot(ai, b)
    si = invert_half(d - dot(cai, b))
    low = dot(si, cai)
    right = dot(aib, si)
    top = jnp.concatenate([ai + dot(aib, low), -right], axis=1)
    return jnp.concatenate([top, jnp.concatenate([-low, si], axis=1)], axis=0)


def eliminate_half(a, reverse):
    tiles = [a[i * TILE : (i + 1) * TILE, :] for i in range(COUNT)]
    order, places = list(range(TILE)), list(range(COUNT))
    if reverse:
        order, places = order[::-1], places[::-1]
    for n, t in enumerate(places):
        rows, forward, inside = step_tile(tiles, t, order)
        tiles[t] = stack(forward)
        for i in places[n + 1 :]:
            tiles[i] = apply_tile(tiles[i], t, rows, inside)
    a = jnp.concatenate(tiles, axis=0)
    rows = lax.broadcasted_iota(jnp.int32, (HB, HB), 0)
    cols = lax.broadcasted_iota(jnp.int32, (HB, HB), 1)
    diag = jnp.sum(jnp.where(rows == cols, a, 0.0), axis=1, keepdims=True)
    scale = 1.0 / jnp.sqrt(diag)
    keep = rows >= cols if reverse else rows <= cols
    factor = jnp.where(keep, a, 0.0) * scale
    inverse = jnp.where(keep, jnp.where(rows == cols, 1.0, 0.0), a) * scale
    return factor, inverse


def factor_kernel(reverse, g_ref, o_ref):
    write_factor(reverse, g_ref[...], o_ref)


def write_factor(reverse, g, o_ref):
    a, b = g[:HB, :HB], g[:HB, HB:]
    c, d = g[HB:, :HB], g[HB:, HB:]
    zero = jnp.zeros((HB, HB), jnp.float32)
    if reverse:
        f2, inv2 = eliminate_half(d, True)
        low = dot(inv2, c)
        f1, _ = eliminate_half(a - dot(low, low, 0, 0), True)
        o_ref[...] = jnp.concatenate(
            [jnp.concatenate([f1, zero], axis=1), jnp.concatenate([low, f2], axis=1)], axis=0
        )
    else:
        f1, inv1 = eliminate_half(a, False)
        up = dot(inv1, b)
        f2, _ = eliminate_half(d - dot(up, up, 0, 0), False)
        o_ref[...] = jnp.concatenate(
            [jnp.concatenate([f1, up], axis=1), jnp.concatenate([zero, f2], axis=1)], axis=0
        )


VM = pl.BlockSpec(memory_space=pltpu.VMEM)
LIMIT = 48 * 1024 * 1024


def factor(gram, reverse):
    return pl.pallas_call(
        functools.partial(factor_kernel, reverse),
        out_shape=jax.ShapeDtypeStruct((NB, NB), jnp.float32),
        in_specs=[VM],
        out_specs=VM,
        compiler_params=pltpu.CompilerParams(vmem_limit_bytes=LIMIT),
        name="factor_rev" if reverse else "factor_fwd",
    )(gram)


def greet(axis, n):
    me = lax.axis_index(axis)
    barrier = pltpu.get_barrier_semaphore()
    for d in range(1, n):
        pl.semaphore_signal(
            barrier, inc=1, device_id={axis: lax.rem(me + d, n)}, device_id_type=MESH
        )
    pl.semaphore_wait(barrier, n - 1)
    return me


def send_all(axis, n, me, source, target, send_sem, recv_sem):
    copies = []
    for d in range(1, n):
        peer = lax.rem(me + d, n)
        copy = pltpu.make_async_remote_copy(
            src_ref=source(peer),
            dst_ref=target.at[me],
            send_sem=send_sem.at[d - 1],
            recv_sem=recv_sem.at[d - 1],
            device_id={axis: peer},
            device_id_type=MESH,
        )
        copy.start()
        copies.append(copy)
    return copies


def gather_pairs(axis, n, me, source, target, send_sem, recv_sem):
    partner = me + 1 - 2 * lax.rem(me, 2)

    def copy_to(src, slot, index, peer):
        copy = pltpu.make_async_remote_copy(
            src_ref=src,
            dst_ref=target.at[slot],
            send_sem=send_sem.at[index],
            recv_sem=recv_sem.at[index],
            device_id={axis: peer},
            device_id_type=MESH,
        )
        copy.start()
        return copy

    half = n // 2
    first = [copy_to(source, me, d - 1, lax.rem(me + 2 * d, n)) for d in range(1, half)]
    rest = [copy_to(source, me, half - 1, partner)]
    for d in range(1, half):
        first[d - 1].wait_recv()
        slot = lax.rem(me + n - 2 * d, n)
        rest.append(copy_to(target.at[slot], slot, half - 1 + d, partner))
    for copy in first:
        copy.wait_send()
    for copy in rest:
        copy.wait()


def exchange_kernel(axis, n, gather, x_ref, o_ref, send_sem, recv_sem):
    me = greet(axis, n)
    if gather and axis == "col":
        o_ref[me] = x_ref[...]
        gather_pairs(axis, n, me, x_ref, o_ref, send_sem, recv_sem)
        return
    source = (lambda peer: x_ref) if gather else (lambda peer: x_ref.at[peer])
    copies = send_all(axis, n, me, source, o_ref, send_sem, recv_sem)
    o_ref[me] = x_ref[...] if gather else x_ref[me]
    for copy in copies:
        copy.wait()


def exchange(x, axis, gather, collective_id):
    n = lax.axis_size(axis)
    shape = (n,) + x.shape if gather else x.shape
    return pl.pallas_call(
        functools.partial(exchange_kernel, axis, n, gather),
        out_shape=jax.ShapeDtypeStruct(shape, jnp.float32),
        in_specs=[VM],
        out_specs=VM,
        scratch_shapes=[pltpu.SemaphoreType.DMA((n - 1,)), pltpu.SemaphoreType.DMA((n - 1,))],
        compiler_params=pltpu.CompilerParams(
            collective_id=collective_id, has_side_effects=True, vmem_limit_bytes=LIMIT
        ),
        name=("gather_" if gather else "scatter_") + axis + str(collective_id),
    )(x)


def panel_kernel(n_row, n_col, x_ref, t_ref, panel_ref, got_ref, gram_ref, f_ref, mid, *sems):
    s1, r1, s2, r2, s3, r3, s4, r4 = sems
    row, col = lax.axis_index("row"), lax.axis_index("col")
    barrier = pltpu.get_barrier_semaphore()
    for axis, n, me in (("row", n_row, row), ("col", n_col, col)):
        for d in range(1, n):
            pl.semaphore_signal(
                barrier, inc=1, device_id={axis: lax.rem(me + d, n)}, device_id_type=MESH
            )
    pl.semaphore_wait(barrier, n_row + n_col - 2)
    first = send_all("col", n_col, col, lambda peer: x_ref.at[peer], mid, s1, r1)
    mid[col] = x_ref[col]
    for copy in first:
        copy.wait()
    own = panel_ref.at[col]
    own[row] = mid[0]
    second = send_all("row", n_row, row, lambda peer: mid.at[0], own, s2, r2)
    for copy in second:
        copy.wait()
    turned = send_all("row", n_row, row, lambda peer: t_ref.at[peer], got_ref, s3, r3)
    got_ref[row] = t_ref[row]
    gather_pairs("col", n_col, col, own, panel_ref, s4, r4)
    shape = (n_row * x_ref.shape[1], NB)

    def add(i, total):
        part = panel_ref[i].reshape(shape)
        return total + dot(part, part, 0, 0)

    gram = lax.fori_loop(0, n_col, add, jnp.zeros((NB, NB), jnp.float32))
    gram_ref[...] = gram
    write_factor(False, gram, f_ref)
    for copy in turned:
        copy.wait()


def panel_step(x, turned, collective_id):
    n_row, n_col = turned.shape[0], x.shape[0]
    square = jax.ShapeDtypeStruct((NB, NB), jnp.float32)
    sems = [pltpu.SemaphoreType.DMA((n - 1,)) for n in (n_col, n_row, n_row, n_col) for _ in "sr"]
    return pl.pallas_call(
        functools.partial(panel_kernel, n_row, n_col),
        out_shape=[
            jax.ShapeDtypeStruct((n_col, n_row) + x.shape[1:], jnp.float32),
            jax.ShapeDtypeStruct(turned.shape, jnp.float32),
            square,
            square,
        ],
        in_specs=[VM, VM],
        out_specs=[VM] * 4,
        scratch_shapes=[pltpu.VMEM(x.shape, jnp.float32)] + sems,
        compiler_params=pltpu.CompilerParams(
            collective_id=collective_id, has_side_effects=True, vmem_limit_bytes=LIMIT
        ),
        name="panel_step",
    )(x, turned)


def solve_kernel(n, z_ref, m_ref, o_ref, s, r):
    me = greet("row", n)
    o_ref[me] = dot(z_ref[...], invert(m_ref[...]))
    for copy in send_all("row", n, me, lambda peer: o_ref.at[me], o_ref, s, r):
        copy.wait()


def solve_gather(z, m, collective_id):
    n = lax.axis_size("row")
    out = pl.pallas_call(
        functools.partial(solve_kernel, n),
        out_shape=jax.ShapeDtypeStruct((n,) + z.shape, jnp.float32),
        in_specs=[VM, VM],
        out_specs=VM,
        scratch_shapes=[pltpu.SemaphoreType.DMA((n - 1,))] * 2,
        compiler_params=pltpu.CompilerParams(
            collective_id=collective_id, has_side_effects=True, vmem_limit_bytes=LIMIT
        ),
        name="solve_row",
    )(z, m)
    return out.reshape(n * z.shape[0], NB)


def reduce_solve_kernel(axis, n, z_ref, m_ref, o_ref, got, s1, r1, s2, r2):
    me = greet(axis, n)
    copies = send_all(axis, n, me, lambda peer: z_ref.at[peer], got, s1, r1)
    inverse = invert(m_ref[...])
    got[me] = z_ref[me]
    for copy in copies:
        copy.wait()
    total = got[0]
    for i in range(1, n):
        total = total + got[i]
    o_ref[me] = dot(total, inverse)
    if axis == "col":
        gather_pairs(axis, n, me, o_ref.at[me], o_ref, s2, r2)
        return
    for copy in send_all(axis, n, me, lambda peer: o_ref.at[me], o_ref, s2, r2):
        copy.wait()


def reduce_solve(z, m, axis, collective_id):
    n = lax.axis_size(axis)
    parts = z.reshape(n, z.shape[0] // n, NB)
    out = pl.pallas_call(
        functools.partial(reduce_solve_kernel, axis, n),
        out_shape=jax.ShapeDtypeStruct(parts.shape, jnp.float32),
        in_specs=[VM, VM],
        out_specs=VM,
        scratch_shapes=[pltpu.VMEM(parts.shape, jnp.float32)]
        + [pltpu.SemaphoreType.DMA((n - 1,))] * 4,
        compiler_params=pltpu.CompilerParams(
            collective_id=collective_id, has_side_effects=True, vmem_limit_bytes=LIMIT
        ),
        name="solve_" + axis,
    )(parts, m)
    return out.reshape(z.shape)


def local(a_matrix, b_matrix):
    rows, block_cols = a_matrix.shape
    n_row, n_col = lax.axis_size("row"), lax.axis_size("col")
    window = NB * n_row // n_col
    start = block_cols - window
    row_place, col_place = lax.axis_index("row"), lax.axis_index("col")
    strip_b = jnp.where(row_place == n_row - 1, b_matrix[:, start:], 0.0)
    strip_b = lax.psum(strip_b, "row")

    chunk = rows // n_col
    turned = jnp.concatenate([a_matrix.T, b_matrix.T], axis=0)
    turned = turned.reshape(n_row, 2 * block_cols // n_row, rows)
    panel, turned, gram, upper = panel_step(
        a_matrix[:, :NB].reshape(n_col, chunk, NB), turned, 1
    )
    panel = jnp.swapaxes(panel, 0, 1).reshape(n_row * rows, NB)
    own_panel = lax.dynamic_slice_in_dim(panel, row_place * rows, rows, 0)
    top = panel[:NB]
    v_rows = own_panel + jnp.where(row_place == 0, upper, 0.0)
    v_full = jnp.concatenate([top + upper, panel[NB:]], axis=0).reshape(n_row, rows, NB)
    z_left = sum(dot(turned[r], v_full[r]) for r in range(n_row))
    left = solve_gather(z_left, gram + dot(top, upper, 0, 0), 4)
    left_a, left_b = left[:block_cols], left[block_cols:]
    last_rows = panel[(n_row - 1) * rows :]
    strip = strip_b - dot(last_rows, left_b[start:], 1, 1)
    strips = exchange(strip, "col", True, 5)
    a_left = a_matrix - dot(v_rows, left_a, 1, 1)
    b_left = b_matrix - dot(v_rows, left_b, 1, 1)

    full = jnp.swapaxes(strips, 0, 1).reshape(NB, n_col * window)
    gram_right = dot(full, full, 1, 1)
    right = factor(gram_right, True)
    m_right = gram_right + dot(full[:, n_col * window - NB :], right)
    n_last = NB // window
    place = col_place - (n_col - n_last)
    added = lax.dynamic_slice_in_dim(right, jnp.maximum(place, 0) * window, window, 0)
    v_cols = strip + jnp.where(place >= 0, added, 0.0).T
    z_right = jnp.concatenate(
        [dot(a_left[:, start:], v_cols, 1, 1), dot(b_left[:, start:], v_cols, 1, 1)], axis=0
    )
    coeff = reduce_solve(z_right, m_right, "col", 6)
    fix = dot(coeff, v_cols)
    a_result = jnp.concatenate([a_left[:, :start], a_left[:, start:] - fix[:rows]], axis=1)
    b_result = jnp.concatenate([b_left[:, :start], b_left[:, start:] - fix[rows:]], axis=1)
    return (a_result, b_result)


def solution(mesh):
    placed = (P("row", "col"), P("row", "col"))
    return jax.shard_map(
        local,
        mesh=mesh,
        in_specs=placed,
        out_specs=(P("row", "col"), P("row", "col")),
        check_vma=False,
    )
```
